512 devices in a mesh: shot: 16 (over y, z_lo), seq: 32 (over z_hi, x, core).
Axes of the slice: x: 4, y: 8, z: 8 (z_hi: 4, z_lo: 2; z = z_hi * 2 + z_lo), core: 2. Of those that a mesh axis runs over, the one named last changes fastest.
Arguments:
- queries: bfloat16 [16, 4096, 1536], P('shot', 'seq'), may hold values from -120 to 120
- key_rows: bfloat16 [16, 4096, 1536], P('shot', 'seq'), may hold values from -6 to 6
- values: bfloat16 [16, 4096, 1536], P('shot', 'seq'), may hold values from -6 to 6
- shot_len: int32 [16], replicated, may hold values from 128 to 4096, as said below
- anchor_len: int32 [16], replicated, may hold values from 16 to 64, as said below
- shot_group: int32 [16], replicated, may hold values from 0 to 1
Outputs:
- attended: bfloat16 [16, 4096, 1536], P('shot', 'seq')
The draws below stay inside these ranges and needn't reach their ends.
Inputs may be any that keep to these rules, and one draw needn't show every extreme that they name: `shot_len`: each a multiple of 128; in every draw some shot has all 4096 slots live. `anchor_len`: in every draw some shot has 64 anchor tokens.
All inputs are finite; a program needn't handle non-finite values.
Results may differ from the reference program's by a relative error of at most 0.0036.
Values may be sent and summed in bfloat16 or wider, within the bound.
A program may use at most 64 MiB of HBM per device.

```python
import math
import jax
import jax.numpy as jnp
from jax import lax

HEADS = 12
HDIM = 128
ANCH = 64
GROUPS = 2
SHOTS = 16
SHOT_LEN = 4096


def draw_queries(key, part):
    key = jax.random.fold_in(key, 1)
    drawn = 2.0 * jax.random.truncated_normal(key, -4.0, 4.0, (SHOTS, SHOT_LEN, HEADS * HDIM), jnp.float32)
    return drawn.astype(jnp.bfloat16)


def draw_key_rows(key, part):
    key = jax.random.fold_in(key, 2)
    drawn = jax.random.truncated_normal(key, -4.0, 4.0, (SHOTS, SHOT_LEN, HEADS * HDIM), jnp.float32)
    return drawn.astype(jnp.bfloat16)


def draw_shot_len(key, part):
    key = jax.random.fold_in(key, 5)
    units = SHOT_LEN // 128
    first = jax.random.randint(jax.random.fold_in(key, 1), (SHOTS,), 1, units + 1)
    second = jax.random.randint(jax.random.fold_in(key, 2), (SHOTS,), 1, units + 1)
    chosen = jax.random.randint(jax.random.fold_in(key, 3), (), 0, SHOTS)
    counts = jnp.minimum(first, second)
    counts = jnp.where(jnp.arange(SHOTS, dtype=jnp.int32) == chosen, units, counts)
    return (counts * 128).astype(jnp.int32)


def draw_anchor_len(key, part):
    key = jax.random.fold_in(key, 9)
    lowest = max(1, ANCH // 4)
    counts = jax.random.randint(jax.random.fold_in(key, 1), (SHOTS,), lowest, ANCH + 1)
    chosen = jax.random.randint(jax.random.fold_in(key, 2), (), 0, SHOTS)
    counts = jnp.where(jnp.arange(SHOTS, dtype=jnp.int32) == chosen, ANCH, counts)
    return counts.astype(jnp.int32)


def touch_ends(entries, rng, low, largest):
    spot = [jax.random.randint(jax.random.fold_in(rng, axis), (), 0, length) for axis, length in enumerate(entries.shape)]
    main_axis = entries.shape.index(max(entries.shape))
    neighbour = spot[:main_axis] + [(spot[main_axis] + 1) % entries.shape[main_axis]] + spot[main_axis + 1:]
    return entries.at[tuple(spot)].set(low).at[tuple(neighbour)].set(largest)


def shard_levels(own_key, dims, pieces, low, top_value):
    level = 1.0
    for axis_at, blocks in pieces:
        steps = jax.random.uniform(jax.random.fold_in(jax.random.fold_in(own_key, 6), axis_at), (blocks,), jnp.float32, low / len(pieces), top_value / len(pieces))
        level = level * jnp.repeat(jnp.exp(steps), dims[axis_at] // blocks).reshape((-1,) + (1,) * (len(dims) - 1 - axis_at))
    return level


def bell_draw(stream_key, dims, spread, limit, pieces=(), kind=jnp.bfloat16):
    entries = jax.random.normal(stream_key, dims, jnp.float32) * spread
    if len(pieces) > 0:
        entries = shard_levels(stream_key, dims, pieces, -0.22, 0.18) * entries
    return jnp.clip(entries, min=-limit, max=limit).astype(kind)


def setup_inputs(seed: int = 0) -> dict:
    key_of = jax.random.split(jax.random.key(seed), 7)
    queries = draw_queries(jax.random.fold_in(key_of[6], 71), 0)
    key_rows = draw_key_rows(jax.random.fold_in(key_of[6], 71), 0)
    values = bell_draw(key_of[2], (SHOTS, SHOT_LEN, HEADS * HDIM), 1.0, 6.0, ((0, 16), (1, 32)))
    shot_len = draw_shot_len(jax.random.fold_in(key_of[6], 71), 0)
    anchor_len = draw_anchor_len(jax.random.fold_in(key_of[6], 71), 0)
    shot_group = touch_ends(jax.random.randint(key_of[5], (SHOTS,), 0, GROUPS), jax.random.fold_in(key_of[5], 1), 0, GROUPS - 1).astype(jnp.int32)
    return dict(queries=queries, key_rows=key_rows, values=values, shot_len=shot_len, anchor_len=anchor_len, shot_group=shot_group)


def reference(queries, key_rows, values, shot_len, anchor_len, shot_group):
    col_total = HEADS * HDIM
    score_scale = 1.0 / math.sqrt(HDIM)
    slot_ids = jnp.arange(SHOT_LEN, dtype=jnp.int32)
    anchor_ids = jnp.arange(ANCH, dtype=jnp.int32)
    shot_ids = jnp.arange(SHOTS, dtype=jnp.int32)
    anchor_keys = key_rows[:, :ANCH].reshape(SHOTS * ANCH, HEADS, HDIM).astype(jnp.float32)
    anchor_vals = values[:, :ANCH].reshape(SHOTS * ANCH, HEADS, HDIM).astype(jnp.float32)
    anchor_live = anchor_ids[None, :] < anchor_len[:, None]
    row_block = math.gcd(SHOT_LEN, 512)

    def one_shot(shot_index):
        own_keys = key_rows[shot_index].reshape(SHOT_LEN, HEADS, HDIM).astype(jnp.float32)
        own_vals = values[shot_index].reshape(SHOT_LEN, HEADS, HDIM).astype(jnp.float32)
        all_keys = jnp.concatenate([own_keys, anchor_keys], axis=0)
        all_vals = jnp.concatenate([own_vals, anchor_vals], axis=0)
        reach = anchor_live & (shot_group == shot_group[shot_index])[:, None] & (shot_ids != shot_index)[:, None]
        key_live = jnp.concatenate([slot_ids < shot_len[shot_index], reach.reshape(SHOTS * ANCH)])
        query_blocks = queries[shot_index].reshape(SHOT_LEN // row_block, row_block, HEADS, HDIM)

        def one_block(query_block):
            scores = jnp.einsum('qhd,khd->hqk', query_block.astype(jnp.float32), all_keys) * score_scale
            scores = jnp.where(key_live[None, None, :], scores, -jnp.inf)
            row_top = lax.optimization_barrier(jnp.max(scores, axis=2, keepdims=True))
            expo_vals = jnp.exp(scores - row_top)
            row_total = lax.optimization_barrier(jnp.sum(expo_vals, axis=2))
            weights = lax.optimization_barrier(expo_vals.astype(jnp.bfloat16)).astype(jnp.float32)
            blended = jnp.einsum('hqk,khd->qhd', weights, all_vals)
            return blended / jnp.transpose(row_total)[:, :, None]
        blended = lax.map(one_block, query_blocks).reshape(SHOT_LEN, col_total)
        live_rows = slot_ids < shot_len[shot_index]
        return jnp.where(live_rows[:, None], blended, 0.0).astype(jnp.bfloat16)
    return lax.map(one_shot, shot_ids)
```

```python
import functools
import math

import jax
import jax.numpy as jnp
from jax import lax
from jax.experimental import pallas as pl
from jax.experimental.pallas import tpu as pltpu
from jax.sharding import PartitionSpec as P

MESH = pl.DeviceIdType.MESH
HEADS = 12
HDIM = 128
ANCH = 64
ROWS = 128
CHIPS = 16
SHOTS = 16
GROUP = 1024
QROWS = CHIPS * ROWS
QB = 512
DEAD = -1e30
SCALE = math.log2(math.e) / math.sqrt(HDIM)


def idle_x(zh, zl):
    return 3


def host_x(j, zh, zl):
    return lax.rem(idle_x(zh, zl) + 1 + j, 4)


def kernel(
    len_ref, anch_ref, group_ref, q_ref, k_ref, v_ref, out_ref,
    qbuf, kbuf, vbuf, obuf, sbuf, mbuf, acc,
    send_sem, q_sem, k_sem, v_sem, kf_sem, vf_sem, a_sem, asend_sem, f_sem, os_sem, o_sem,
):
    shot = lax.axis_index("shot")
    seq = lax.axis_index("seq")
    y, zl = shot // 2, shot % 2
    core, x, zh = seq % 2, (seq // 2) % 4, seq // 8
    chip = seq // 2
    place = lax.rem(x - idle_x(zh, zl) - 1 + 8, 4)
    is_host = place < 3
    head = zh * 3 + jnp.minimum(place, 2)

    vbuf[:, :, :, HDIM:] = jnp.ones((20, 2, ROWS, HDIM), jnp.bfloat16)

    sibling = (shot, chip * 2 + 1 - core)

    def mate(t):
        return (shot, t * 2 + core)

    def y_peer(k):
        return (lax.rem(y + k, 8) * 2 + zl, seq)

    partner_x = lax.rem(x - idle_x(zh, zl) + idle_x(zh, 1 - zl) + 8, 4)
    partner = (y * 2 + 1 - zl, (zh * 4 + partner_x) * 2 + core)

    barrier = pltpu.get_barrier_semaphore()

    def greet(device):
        pl.semaphore_signal(barrier, inc=1, device_id=device, device_id_type=MESH)

    lax.fori_loop(1, CHIPS, lambda i, _: (greet(mate(lax.rem(chip + i, CHIPS))), 0)[1], 0)
    lax.fori_loop(1, 8, lambda i, _: (greet(y_peer(i)), 0)[1], 0)
    greet(sibling)
    greet(partner)
    pl.semaphore_wait(barrier, CHIPS - 1 + 7 + 2)

    def remote(src, dst, ssem, rsem, device):
        return pltpu.make_async_remote_copy(
            src_ref=src, dst_ref=dst, send_sem=ssem, recv_sem=rsem,
            device_id=device, device_id_type=MESH,
        )

    def drain(ref, sem):
        pltpu.make_async_copy(ref, ref, sem).wait()

    def to_chip(src, dst, ssem, rsem, t):
        @pl.when(t == chip)
        def _():
            pltpu.make_async_copy(src, dst, rsem).start()

        @pl.when(t != chip)
        def _():
            remote(src, dst, ssem, rsem, mate(t)).start()

    def columns(h):
        return pl.ds(pl.multiple_of(h * HDIM, HDIM), HDIM)

    def anchor_at(buf, t):
        return buf.at[16 + t // 4, (t // 2) % 2, pl.ds(pl.multiple_of((t % 2) * ANCH, ANCH), ANCH), pl.ds(0, HDIM)]

    def pair_at(buf, yy):
        return buf.at[16 + yy // 2, yy % 2, :, pl.ds(0, HDIM)]

    @pl.when(seq == 0)
    def _():
        def one(h, _):
            t = (h // 3) * 4 + host_x(h % 3, h // 3, zl)
            to_chip(k_ref.at[pl.ds(0, ANCH), columns(h)], anchor_at(kbuf, shot), asend_sem.at[0], a_sem.at[0], t)
            to_chip(v_ref.at[pl.ds(0, ANCH), columns(h)], anchor_at(vbuf, shot), asend_sem.at[0], a_sem.at[1], t)
            return 0

        lax.fori_loop(0, HEADS, one, 0)

    def send_all(kind):
        def one(i, _):
            far = (2 + 3 * ((i // 3) * (i // 3 + 1) // 2)) % 4
            z = lax.rem(zh + far, 4)
            j = lax.rem(x + i, 3)
            h = z * 3 + j
            t = z * 4 + host_x(j, z, zl)
            if kind == 0:
                to_chip(q_ref.at[:, columns(h)], qbuf.at[chip], send_sem.at[0], q_sem, t)
            elif kind == 1:
                to_chip(k_ref.at[:, columns(h)], kbuf.at[chip, core], send_sem.at[1], k_sem.at[zh], t)
            else:
                to_chip(v_ref.at[:, columns(h)], vbuf.at[chip, core, :, pl.ds(0, HDIM)], send_sem.at[2], v_sem.at[zh], t)
            return 0

        lax.fori_loop(0, HEADS, one, 0)

    send_all(0)
    send_all(1)
    send_all(2)

    @pl.when(is_host)
    def _():
        @pl.when(core == 0)
        def _():
            drain(anchor_at(kbuf, shot), a_sem.at[0])
            drain(anchor_at(vbuf, shot), a_sem.at[1])
            remote(anchor_at(kbuf, shot), anchor_at(kbuf, shot), asend_sem.at[1], a_sem.at[2], partner).start()
            remote(anchor_at(vbuf, shot), anchor_at(vbuf, shot), asend_sem.at[1], a_sem.at[3], partner).start()
            other = y * 2 + 1 - zl
            drain(anchor_at(kbuf, other), a_sem.at[2])
            drain(anchor_at(vbuf, other), a_sem.at[3])

            def one(i, _):
                remote(pair_at(kbuf, y), pair_at(kbuf, y), asend_sem.at[2], a_sem.at[4], y_peer(i)).start()
                remote(pair_at(vbuf, y), pair_at(vbuf, y), asend_sem.at[2], a_sem.at[5], y_peer(i)).start()
                return 0

            lax.fori_loop(1, 8, one, 0)
            arrived = kbuf.at[pl.ds(0, 7), 0]
            drain(arrived, a_sem.at[4])
            drain(arrived, a_sem.at[5])
            all_k = kbuf.at[pl.ds(16, 4)]
            all_v = vbuf.at[pl.ds(16, 4), :, :, pl.ds(0, HDIM)]
            remote(all_k, all_k, asend_sem.at[3], f_sem.at[0], sibling).start()
            remote(all_v, all_v, asend_sem.at[3], f_sem.at[1], sibling).start()

        @pl.when(core == 1)
        def _():
            drain(kbuf.at[pl.ds(16, 4)], f_sem.at[0])
            drain(vbuf.at[pl.ds(16, 4), :, :, pl.ds(0, HDIM)], f_sem.at[1])

        def source(i):
            return lax.rem(zh + (2 + 3 * (i * (i + 1) // 2)) % 4, 4)

        def halves(buf, g, c):
            return buf.at[pl.ds(g * 4, 4), c, :, pl.ds(0, HDIM)]

        def take(buf, sem, fsem, g):
            drain(halves(buf, g, core), sem.at[g])
            remote(halves(buf, g, core), halves(buf, g, core), asend_sem.at[4], fsem.at[g], sibling).start()

        lane = lax.broadcasted_iota(jnp.int32, (8, GROUP), 1)
        mbuf[...] = jnp.full((QROWS, HDIM), DEAD, jnp.float32)

        def scores(slot, keys, bias):
            keys = keys.reshape(GROUP, HDIM)
            for r in range(0, QROWS, QB):
                rows = qbuf[r // ROWS : (r + QB) // ROWS].reshape(QB, HDIM)
                found = lax.dot_general(rows, keys, (((1,), (1,)), ((), ())), preferred_element_type=jnp.float32)
                found = found * SCALE + bias[:1]
                sbuf[slot, r : r + QB, :] = found
                top = mbuf[r : r + QB, :]
                for c in range(0, GROUP, HDIM):
                    top = jnp.maximum(top, found[:, c : c + HDIM])
                mbuf[r : r + QB, :] = top

        drain(qbuf, q_sem)
        limit = jnp.zeros((8, GROUP), jnp.int32)
        my_group = group_ref[shot]
        for t in range(SHOTS):
            seen = jnp.where(jnp.logical_and(group_ref[t] == my_group, shot != t), anch_ref[t], 0)
            limit = jnp.where(lane // ANCH == t, seen, limit)
        scores(4, kbuf[16:20], jnp.where(lane % ANCH < limit, 0.0, DEAD))
        live = len_ref[shot]

        def first(i, _):
            g = source(i)
            take(kbuf, k_sem, kf_sem, g)
            drain(halves(kbuf, g, 1 - core), kf_sem.at[g])
            scores(i, kbuf[pl.ds(g * 4, 4)], jnp.where(lane + g * GROUP < live, 0.0, DEAD))
            return 0

        lax.fori_loop(0, 4, first, 0)
        mbuf[...] = jnp.broadcast_to(jnp.max(mbuf[...], axis=1, keepdims=True), (QROWS, HDIM))

        def product(slot, rows, vals):
            weights = jnp.exp2(sbuf[slot, rows, :] - mbuf[rows, :1]).astype(jnp.bfloat16)
            return jnp.dot(weights, vals, preferred_element_type=jnp.float32)

        vals = vbuf[16:20].reshape(GROUP, 2 * HDIM)
        for r in range(0, QROWS, QB):
            acc[r : r + QB, :] = product(4, pl.ds(r, QB), vals)

        def second(i, _):
            g = source(i)
            take(vbuf, v_sem, vf_sem, g)
            drain(halves(vbuf, g, 1 - core), vf_sem.at[g])
            vals = vbuf[pl.ds(g * 4, 4)].reshape(GROUP, 2 * HDIM)
            for r in range(0, QROWS, QB):
                acc[r : r + QB, :] += product(i, pl.ds(r, QB), vals)
            return 0

        lax.fori_loop(0, 3, second, 0)
        g = source(3)
        take(vbuf, v_sem, vf_sem, g)
        drain(halves(vbuf, g, 1 - core), vf_sem.at[g])
        vals = vbuf[pl.ds(g * 4, 4)].reshape(GROUP, 2 * HDIM)
        for n in range(4):
            z = source(n)
            rows = pl.ds(pl.multiple_of(z * QB, QB), QB)
            done = acc[rows, :] + product(3, rows, vals)
            blended = done[:, :HDIM] / done[:, HDIM:]
            for k in range(4):
                t = z * 4 + k
                slots = (t * 2 + core) * ROWS + lax.broadcasted_iota(jnp.int32, (ROWS, HDIM), 0)
                piece = jnp.where(slots < live, blended[k * ROWS : (k + 1) * ROWS], 0.0)
                obuf[t] = piece.astype(jnp.bfloat16)
                to_chip(obuf.at[t], out_ref.at[:, columns(head)], os_sem, o_sem, t)

        drain(obuf.at[pl.ds(0, 15)], os_sem)

        drain(kbuf.at[pl.ds(0, CHIPS)], asend_sem.at[4])

        @pl.when(core == 0)
        def _():
            drain(kbuf.at[0, 0], asend_sem.at[1])
            drain(kbuf.at[pl.ds(0, 14), 0], asend_sem.at[2])
            drain(kbuf.at[pl.ds(0, 8)], asend_sem.at[3])

    @pl.when(seq == 0)
    def _():
        @pl.when(is_host)
        def _():
            drain(kbuf.at[pl.ds(0, 11), 0], asend_sem.at[0])

        @pl.when(jnp.logical_not(is_host))
        def _():
            drain(kbuf.at[pl.ds(0, 12), 0], asend_sem.at[0])

    for kind in range(3):
        @pl.when(is_host)
        def _():
            drain(q_ref.at[:, pl.ds(0, 11 * HDIM)], send_sem.at[kind])

        @pl.when(jnp.logical_not(is_host))
        def _():
            drain(q_ref, send_sem.at[kind])

    drain(out_ref, o_sem)


def local(queries, key_rows, values, shot_len, anchor_len, shot_group):
    whole = pl.BlockSpec(memory_space=pl.ANY)
    scalars = pl.BlockSpec(memory_space=pltpu.SMEM)
    dma = pltpu.SemaphoreType.DMA
    flat = (ROWS, HEADS * HDIM)
    out = pl.pallas_call(
        kernel,
        out_shape=jax.ShapeDtypeStruct(flat, jnp.bfloat16),
        in_specs=[scalars] * 3 + [whole] * 3,
        out_specs=whole,
        scratch_shapes=[
            pltpu.VMEM((CHIPS, ROWS, HDIM), jnp.bfloat16),
            pltpu.VMEM((20, 2, ROWS, HDIM), jnp.bfloat16),
            pltpu.VMEM((20, 2, ROWS, 2 * HDIM), jnp.bfloat16),
            pltpu.VMEM((CHIPS, ROWS, HDIM), jnp.bfloat16),
            pltpu.VMEM((5, QROWS, GROUP), jnp.float32),
            pltpu.VMEM((QROWS, HDIM), jnp.float32),
            pltpu.VMEM((QROWS, 2 * HDIM), jnp.float32),
            dma((3,)), dma, dma((4,)), dma((4,)), dma((4,)), dma((4,)),
            dma((6,)), dma((5,)), dma((2,)), dma, dma,
        ],
        compiler_params=pltpu.CompilerParams(
            collective_id=0, has_side_effects=True, vmem_limit_bytes=60 * 2**20
        ),
    )(
        shot_len, anchor_len, shot_group,
        queries.reshape(flat), key_rows.reshape(flat), values.reshape(flat),
    )
    return out.reshape(1, *flat)


def solution(mesh):
    spec = P("shot", "seq", None)
    return jax.shard_map(
        local, mesh=mesh, in_specs=(spec, spec, spec, P(), P(), P()), out_specs=spec, check_vma=False
    )
```

```python
import functools
import math

import jax
import jax.numpy as jnp
from jax import lax
from jax.experimental import pallas as pl
from jax.experimental.pallas import tpu as pltpu
from jax.sharding import PartitionSpec as P

MESH = pl.DeviceIdType.MESH
HEADS = 12
HDIM = 128
ANCH = 64
ROWS = 128
CHIPS = 16
SHOTS = 16
GROUP = 1024
QROWS = CHIPS * ROWS
QB = 512
DEAD = -1e30
AHEAD = 3
SCALE = math.log2(math.e) / math.sqrt(HDIM)


def kernel(
    len_ref, anch_ref, group_ref, q_ref, k_ref, v_ref, out_ref,
    qbuf, kbuf, vbuf, obuf, sbuf, mbuf,
    send_sem, q_sem, k_sem, v_sem, kf_sem, vf_sem, a_sem, asend_sem, f_sem, os_sem, o_sem,
):
    shot = lax.axis_index("shot")
    seq = lax.axis_index("seq")
    y, zl = shot // 2, shot % 2
    core, x, zh = seq % 2, (seq // 2) % 4, seq // 8
    here = x * 4 + zh
    is_host = x < 3
    head = zh * 3 + jnp.minimum(x, 2)

    vbuf[:, :, :, HDIM:] = jnp.ones((20, 2, ROWS, HDIM), jnp.bfloat16)

    sibling = (shot, seq + 1 - 2 * core)

    def mate(t):
        return (shot, (lax.rem(t, 4) * 4 + t // 4) * 2 + core)

    def y_peer(k):
        return (lax.rem(y + k, 8) * 2 + zl, seq)

    partner = (y * 2 + 1 - zl, seq)

    barrier = pltpu.get_barrier_semaphore()

    def greet(device):
        pl.semaphore_signal(barrier, inc=1, device_id=device, device_id_type=MESH)

    lax.fori_loop(1, CHIPS, lambda i, _: (greet(mate(lax.rem(here + i, CHIPS))), 0)[1], 0)
    lax.fori_loop(1, 8, lambda i, _: (greet(y_peer(i)), 0)[1], 0)
    greet(sibling)
    greet(partner)
    pl.semaphore_wait(barrier, CHIPS - 1 + 7 + 2)

    def remote(src, dst, ssem, rsem, device):
        return pltpu.make_async_remote_copy(
            src_ref=src, dst_ref=dst, send_sem=ssem, recv_sem=rsem,
            device_id=device, device_id_type=MESH,
        )

    def drain(ref, sem):
        pltpu.make_async_copy(ref, ref, sem).wait()

    def to_chip(src, dst, ssem, rsem, t):
        @pl.when(t == here)
        def _():
            pltpu.make_async_copy(src, dst, rsem).start()

        @pl.when(t != here)
        def _():
            remote(src, dst, ssem, rsem, mate(t)).start()

    def columns(h):
        return pl.ds(pl.multiple_of(h * HDIM, HDIM), HDIM)

    def anchor_at(buf, t):
        return buf.at[16 + t // 4, (t // 2) % 2, pl.ds(pl.multiple_of((t % 2) * ANCH, ANCH), ANCH), pl.ds(0, HDIM)]

    def pair_at(buf, yy):
        return buf.at[16 + yy // 2, yy % 2, :, pl.ds(0, HDIM)]

    @pl.when(seq == 0)
    def _():
        def one(h, _):
            t = lax.rem(h, 3) * 4 + h // 3
            to_chip(k_ref.at[pl.ds(0, ANCH), columns(h)], anchor_at(kbuf, shot), asend_sem.at[0], a_sem.at[0], t)
            to_chip(v_ref.at[pl.ds(0, ANCH), columns(h)], anchor_at(vbuf, shot), asend_sem.at[0], a_sem.at[1], t)
            return 0

        lax.fori_loop(0, HEADS, one, 0)

    def send(kind, turn):
        to_x = lax.rem(x + turn, 3)

        def one(n, _):
            z = lax.rem(zh + 2 + 3 * n, 4)
            h = z * 3 + to_x
            t = to_x * 4 + z
            if kind == 0:
                to_chip(q_ref.at[:, columns(h)], qbuf.at[here], send_sem.at[0, turn], q_sem, t)
            elif kind == 1:
                to_chip(k_ref.at[:, columns(h)], kbuf.at[here, core], send_sem.at[1, turn], k_sem.at[x], t)
            else:
                to_chip(v_ref.at[:, columns(h)], vbuf.at[here, core, :, pl.ds(0, HDIM)], send_sem.at[2, turn], v_sem.at[x], t)
            return 0

        lax.fori_loop(0, 4, one, 0)

    def sent(kind, turn):
        stayed = jnp.logical_and(turn == 0, is_host)

        @pl.when(jnp.logical_not(stayed))
        def _():
            drain(q_ref.at[:, pl.ds(0, 4 * HDIM)], send_sem.at[kind, turn])

        @pl.when(stayed)
        def _():
            drain(q_ref.at[:, pl.ds(0, 3 * HDIM)], send_sem.at[kind, turn])

    def send_next(n):
        sent((n - AHEAD) // 3, (n - AHEAD) % 3)
        send(n // 3, n % 3)

    for n in range(AHEAD):
        send(n // 3, n % 3)

    @pl.when(jnp.logical_not(is_host))
    def _():
        for n in range(AHEAD, 9):
            send_next(n)

    @pl.when(is_host)
    def _():
        all_k = kbuf.at[pl.ds(16, 4)]
        all_v = vbuf.at[pl.ds(16, 4), :, :, pl.ds(0, HDIM)]

        def anchors_to_partner():
            drain(anchor_at(kbuf, shot), a_sem.at[0])
            drain(anchor_at(vbuf, shot), a_sem.at[1])
            remote(anchor_at(kbuf, shot), anchor_at(kbuf, shot), asend_sem.at[1], a_sem.at[2], partner).start()
            remote(anchor_at(vbuf, shot), anchor_at(vbuf, shot), asend_sem.at[1], a_sem.at[3], partner).start()

        def anchors_to_peers():
            other = y * 2 + 1 - zl
            drain(anchor_at(kbuf, other), a_sem.at[2])
            drain(anchor_at(vbuf, other), a_sem.at[3])

            def one(i, _):
                remote(pair_at(kbuf, y), pair_at(kbuf, y), asend_sem.at[2], a_sem.at[4], y_peer(i)).start()
                remote(pair_at(vbuf, y), pair_at(vbuf, y), asend_sem.at[2], a_sem.at[5], y_peer(i)).start()
                return 0

            lax.fori_loop(1, 8, one, 0)

        def anchors_to_sibling():
            arrived = kbuf.at[pl.ds(0, 7), 0]
            drain(arrived, a_sem.at[4])
            drain(arrived, a_sem.at[5])
            remote(all_k, all_k, asend_sem.at[3], f_sem.at[0], sibling).start()
            remote(all_v, all_v, asend_sem.at[3], f_sem.at[1], sibling).start()

        @pl.when(core == 0)
        def _():
            anchors_to_partner()

        send_next(3)

        @pl.when(core == 0)
        def _():
            anchors_to_peers()

        send_next(4)
        send_next(5)

        def source(i):
            return lax.rem(x + 4 - i, 4)

        def halves(buf, g, c):
            return buf.at[pl.ds(g * 4, 4), c, :, pl.ds(0, HDIM)]

        def take(buf, sem, fsem, g):
            drain(halves(buf, g, core), sem.at[g])
            remote(halves(buf, g, core), halves(buf, g, core), asend_sem.at[4], fsem.at[g], sibling).start()

        lane = lax.broadcasted_iota(jnp.int32, (8, GROUP), 1)
        mbuf[...] = jnp.full((QROWS, HDIM), DEAD, jnp.float32)

        def scores(slot, keys, bias):
            keys = keys.reshape(GROUP, HDIM)
            for r in range(0, QROWS, QB):
                rows = qbuf[r // ROWS : (r + QB) // ROWS].reshape(QB, HDIM)
                found = lax.dot_general(rows, keys, (((1,), (1,)), ((), ())), preferred_element_type=jnp.float32)
                found = found * SCALE + bias[:1]
                sbuf[slot, r : r + QB, :] = found
                top = mbuf[r : r + QB, :]
                for c in range(0, GROUP, HDIM):
                    top = jnp.maximum(top, found[:, c : c + HDIM])
                mbuf[r : r + QB, :] = top

        drain(qbuf, q_sem)

        live = len_ref[shot]

        def first(i, _):
            g = source(i)

            @pl.when(i == 0)
            def _():
                send_next(6)

            @pl.when(i == 1)
            def _():
                send_next(7)

            @pl.when(i == 2)
            def _():
                send_next(8)

            take(kbuf, k_sem, kf_sem, g)

            @pl.when(jnp.logical_and(core == 0, i == 3))
            def _():
                anchors_to_sibling()

            drain(halves(kbuf, g, 1 - core), kf_sem.at[g])
            slot = ((lane // (2 * ROWS)) * 4 + g) * (2 * ROWS) + lane % (2 * ROWS)
            scores(i, kbuf[pl.ds(g * 4, 4)], jnp.where(slot < live, 0.0, DEAD))
            return 0

        lax.fori_loop(0, 4, first, 0)
        limit = jnp.zeros((8, GROUP), jnp.int32)
        my_group = group_ref[shot]
        for t in range(SHOTS):
            seen = jnp.where(jnp.logical_and(group_ref[t] == my_group, shot != t), anch_ref[t], 0)
            limit = jnp.where(lane // ANCH == t, seen, limit)

        @pl.when(core == 1)
        def _():
            drain(all_k, f_sem.at[0])
            drain(all_v, f_sem.at[1])

        scores(4, kbuf[16:20], jnp.where(lane % ANCH < limit, 0.0, DEAD))
        mbuf[...] = jnp.broadcast_to(jnp.max(mbuf[...], axis=1, keepdims=True), (QROWS, HDIM))

        lax.fori_loop(0, 4, lambda i, _: (take(vbuf, v_sem, vf_sem, source(i)), 0)[1], 0)
        lax.fori_loop(0, 4, lambda i, _: (drain(halves(vbuf, i, 1 - core), vf_sem.at[i]), 0)[1], 0)

        def product(slot, rows, first):
            weights = jnp.exp2(sbuf[slot, rows, :] - mbuf[rows, :1]).astype(jnp.bfloat16)
            vals = vbuf[pl.ds(first, 4)].reshape(GROUP, 2 * HDIM)
            return jnp.dot(weights, vals, preferred_element_type=jnp.float32)

        for n in range(4):
            to_x = lax.rem(x + n + 1, 4)
            rows = pl.ds(pl.multiple_of(to_x * QB, QB), QB)
            done = product(4, rows, 16)
            for i in range(4):
                done += product(i, rows, source(i) * 4)
            blended = done[:, :HDIM] / done[:, HDIM:]
            for k in range(4):
                t = to_x * 4 + k
                slots = ((k * 4 + to_x) * 2 + core) * ROWS + lax.broadcasted_iota(jnp.int32, (ROWS, HDIM), 0)
                piece = jnp.where(slots < live, blended[k * ROWS : (k + 1) * ROWS], 0.0)
                obuf[t] = piece.astype(jnp.bfloat16)
                to_chip(obuf.at[t], out_ref.at[:, columns(head)], os_sem, o_sem, t)

        drain(obuf.at[pl.ds(0, 15)], os_sem)

        drain(kbuf.at[pl.ds(0, CHIPS)], asend_sem.at[4])

        @pl.when(core == 0)
        def _():
            drain(kbuf.at[0, 0], asend_sem.at[1])
            drain(kbuf.at[pl.ds(0, 14), 0], asend_sem.at[2])
            drain(kbuf.at[pl.ds(0, 8)], asend_sem.at[3])

    @pl.when(seq == 0)
    def _():
        @pl.when(is_host)
        def _():
            drain(kbuf.at[pl.ds(0, 11), 0], asend_sem.at[0])

        @pl.when(jnp.logical_not(is_host))
        def _():
            drain(kbuf.at[pl.ds(0, 12), 0], asend_sem.at[0])

    for n in range(9 - AHEAD, 9):
        sent(n // 3, n % 3)
    drain(out_ref, o_sem)


def local(queries, key_rows, values, shot_len, anchor_len, shot_group):
    whole = pl.BlockSpec(memory_space=pl.ANY)
    scalars = pl.BlockSpec(memory_space=pltpu.SMEM)
    dma = pltpu.SemaphoreType.DMA
    flat = (ROWS, HEADS * HDIM)
    out = pl.pallas_call(
        kernel,
        out_shape=jax.ShapeDtypeStruct(flat, jnp.bfloat16),
        in_specs=[scalars] * 3 + [whole] * 3,
        out_specs=whole,
        scratch_shapes=[
            pltpu.VMEM((CHIPS, ROWS, HDIM), jnp.bfloat16),
            pltpu.VMEM((20, 2, ROWS, HDIM), jnp.bfloat16),
            pltpu.VMEM((20, 2, ROWS, 2 * HDIM), jnp.bfloat16),
            pltpu.VMEM((CHIPS, ROWS, HDIM), jnp.bfloat16),
            pltpu.VMEM((5, QROWS, GROUP), jnp.float32),
            pltpu.VMEM((QROWS, HDIM), jnp.float32),
            dma((3, 3)), dma, dma((4,)), dma((4,)), dma((4,)), dma((4,)),
            dma((6,)), dma((5,)), dma((2,)), dma, dma,
        ],
        compiler_params=pltpu.CompilerParams(
            collective_id=0, has_side_effects=True, vmem_limit_bytes=60 * 2**20
        ),
    )(
        shot_len, anchor_len, shot_group,
        queries.reshape(flat), key_rows.reshape(flat), values.reshape(flat),
    )
    return out.reshape(1, *flat)


def solution(mesh):
    spec = P("shot", "seq", None)
    return jax.shard_map(
        local, mesh=mesh, in_specs=(spec, spec, spec, P(), P(), P()), out_specs=spec, check_vma=False
    )
```

```python
import functools
import math

import jax
import jax.numpy as jnp
from jax import lax
from jax.experimental import pallas as pl
from jax.experimental.pallas import tpu as pltpu
from jax.sharding import PartitionSpec as P

MESH = pl.DeviceIdType.MESH
HEADS = 12
HDIM = 128
ANCH = 64
ROWS = 128
CHIPS = 16
SHOTS = 16
GROUP = 512
QROWS = CHIPS * ROWS
QB = 512
DEAD = -1e30
AHEAD = 3
SCALE = math.log2(math.e) / math.sqrt(HDIM)


def kernel(
    len_ref, anch_ref, group_ref, q_ref, k_ref, v_ref, out_ref,
    qbuf, kbuf, vbuf, obuf, sbuf, mbuf, first_vals,
    send_sem, q_sem, k_sem, v_sem, kf_sem, vf_sem, a_sem, asend_sem, f_sem, os_sem, o_sem,
):
    shot = lax.axis_index("shot")
    seq = lax.axis_index("seq")
    y, zl = shot // 2, shot % 2
    core, x, zh = seq % 2, (seq // 2) % 4, seq // 8
    here = x * 4 + zh
    is_host = x < 3
    head = zh * 3 + jnp.minimum(x, 2)

    vbuf[:, :, :, HDIM:] = jnp.ones((2, 20, ROWS, HDIM), jnp.bfloat16)

    sibling = (shot, seq + 1 - 2 * core)

    def mate(t):
        return (shot, (lax.rem(t, 4) * 4 + t // 4) * 2 + core)

    def y_peer(k):
        return (lax.rem(y + k, 8) * 2 + zl, seq)

    partner = (y * 2 + 1 - zl, seq)

    barrier = pltpu.get_barrier_semaphore()

    def greet(device):
        pl.semaphore_signal(barrier, inc=1, device_id=device, device_id_type=MESH)

    lax.fori_loop(1, CHIPS, lambda i, _: (greet(mate(lax.rem(here + i, CHIPS))), 0)[1], 0)
    lax.fori_loop(1, 8, lambda i, _: (greet(y_peer(i)), 0)[1], 0)
    greet(sibling)
    greet(partner)
    pl.semaphore_wait(barrier, CHIPS - 1 + 7 + 2)

    def remote(src, dst, ssem, rsem, device):
        return pltpu.make_async_remote_copy(
            src_ref=src, dst_ref=dst, send_sem=ssem, recv_sem=rsem,
            device_id=device, device_id_type=MESH,
        )

    def drain(ref, sem):
        pltpu.make_async_copy(ref, ref, sem).wait()

    def to_chip(src, dst, ssem, rsem, t):
        @pl.when(t == here)
        def _():
            pltpu.make_async_copy(src, dst, rsem).start()

        @pl.when(t != here)
        def _():
            remote(src, dst, ssem, rsem, mate(t)).start()

    def columns(h):
        return pl.ds(pl.multiple_of(h * HDIM, HDIM), HDIM)

    def anchor_at(buf, t):
        return buf.at[(t // 2) % 2, 16 + t // 4, pl.ds(pl.multiple_of((t % 2) * ANCH, ANCH), ANCH), pl.ds(0, HDIM)]

    def pair_at(buf, yy):
        return buf.at[yy % 2, 16 + yy // 2, :, pl.ds(0, HDIM)]

    def anchors_out(src, buf):
        def one(h, _):
            to_chip(src.at[pl.ds(0, ANCH), columns(h)], anchor_at(buf, shot), asend_sem.at[0], a_sem.at[0], lax.rem(h, 3) * 4 + h // 3)
            return 0

        lax.fori_loop(0, HEADS, one, 0)

    @pl.when(seq == 0)
    def _():
        remote(v_ref.at[pl.ds(0, ANCH)], first_vals, asend_sem.at[5], a_sem.at[3], sibling).start()
        anchors_out(k_ref, kbuf)

    def send(kind, turn):
        to_x = lax.rem(x + turn, 3)

        def one(n, _):
            z = lax.rem(zh + 2 + 3 * n, 4)
            h = z * 3 + to_x
            t = to_x * 4 + z
            if kind == 0:
                to_chip(q_ref.at[:, columns(h)], qbuf.at[here], send_sem.at[0, turn], q_sem, t)
            elif kind == 1:
                to_chip(k_ref.at[:, columns(h)], kbuf.at[core, here], send_sem.at[1, turn], k_sem.at[x], t)
            else:
                to_chip(v_ref.at[:, columns(h)], vbuf.at[core, here, :, pl.ds(0, HDIM)], send_sem.at[2, turn], v_sem.at[x], t)
            return 0

        lax.fori_loop(0, 4, one, 0)

    def sent(kind, turn):
        stayed = jnp.logical_and(turn == 0, is_host)

        @pl.when(jnp.logical_not(stayed))
        def _():
            drain(q_ref.at[:, pl.ds(0, 4 * HDIM)], send_sem.at[kind, turn])

        @pl.when(stayed)
        def _():
            drain(q_ref.at[:, pl.ds(0, 3 * HDIM)], send_sem.at[kind, turn])

    def send_next(n):
        sent((n - AHEAD) // 3, (n - AHEAD) % 3)
        send(n // 3, n % 3)

    for n in range(AHEAD):
        send(n // 3, n % 3)

    @pl.when(seq == 1)
    def _():
        drain(first_vals, a_sem.at[3])
        anchors_out(first_vals, vbuf)

    @pl.when(jnp.logical_not(is_host))
    def _():
        for n in range(AHEAD, 9):
            send_next(n)

    @pl.when(is_host)
    def _():
        all_k = kbuf.at[:, pl.ds(16, 4)]
        all_v = vbuf.at[:, pl.ds(16, 4), :, pl.ds(0, HDIM)]

        def anchors_to_partner(buf):
            drain(anchor_at(buf, shot), a_sem.at[0])
            remote(anchor_at(buf, shot), anchor_at(buf, shot), asend_sem.at[1], a_sem.at[1], partner).start()

        def anchors_to_peers(buf):
            drain(anchor_at(buf, y * 2 + 1 - zl), a_sem.at[1])

            def one(i, _):
                remote(pair_at(buf, y), pair_at(buf, y), asend_sem.at[2], a_sem.at[2], y_peer(i)).start()
                return 0

            lax.fori_loop(1, 8, one, 0)

        def anchors_to_sibling(part):
            drain(kbuf.at[0, pl.ds(0, 7)], a_sem.at[2])
            remote(part, part, asend_sem.at[3], f_sem, sibling).start()

        def by_core(step, keys, vals):
            @pl.when(core == 0)
            def _():
                step(keys)

            @pl.when(core == 1)
            def _():
                step(vals)

        by_core(anchors_to_partner, kbuf, vbuf)
        send_next(3)
        by_core(anchors_to_peers, kbuf, vbuf)
        send_next(4)
        send_next(5)

        def source(i):
            return lax.rem(x + 4 - i, 4)

        def halves(buf, g, c):
            return buf.at[c, pl.ds(g * 4, 4), :, pl.ds(0, HDIM)]

        def take(buf, sem, fsem, g):
            drain(halves(buf, g, core), sem.at[g])
            remote(halves(buf, g, core), halves(buf, g, core), asend_sem.at[4], fsem.at[g], sibling).start()

        lane = lax.broadcasted_iota(jnp.int32, (8, GROUP), 1)
        mbuf[...] = jnp.full((QROWS, HDIM), DEAD, jnp.float32)

        def scores(slot, keys, bias):
            keys = keys.reshape(GROUP, HDIM)
            for r in range(0, QROWS, QB):
                rows = qbuf[r // ROWS : (r + QB) // ROWS].reshape(QB, HDIM)
                found = lax.dot_general(rows, keys, (((1,), (1,)), ((), ())), preferred_element_type=jnp.float32)
                found = found * SCALE + bias[:1]
                sbuf[slot, r : r + QB, :] = found
                top = mbuf[r : r + QB, :]
                for c in range(0, GROUP, HDIM):
                    top = jnp.maximum(top, found[:, c : c + HDIM])
                mbuf[r : r + QB, :] = top

        drain(qbuf, q_sem)

        live = len_ref[shot]

        def first(i, _):
            g = source(i)

            @pl.when(i == 0)
            def _():
                send_next(6)

            @pl.when(i == 1)
            def _():
                send_next(7)

            @pl.when(i == 2)
            def _():
                send_next(8)

            take(kbuf, k_sem, kf_sem, g)

            @pl.when(i == 3)
            def _():
                by_core(anchors_to_sibling, all_k, all_v)


            def half(c):
                slot = ((lane // ROWS) * 4 + g) * (2 * ROWS) + c * ROWS + lane % ROWS
                scores(2 * i + jnp.where(c == core, 0, 1), kbuf[c, pl.ds(g * 4, 4)], jnp.where(slot < live, 0.0, DEAD))

            half(core)
            drain(halves(kbuf, g, 1 - core), kf_sem.at[g])
            half(1 - core)
            return 0

        lax.fori_loop(0, 4, first, 0)
        my_group = group_ref[shot]

        @pl.when(core == 1)
        def _():
            drain(all_k, f_sem)

        for c in range(2):
            limit = jnp.zeros((8, GROUP), jnp.int32)
            for n in range(SHOTS // 2):
                t = (n // 2) * 4 + c * 2 + n % 2
                seen = jnp.where(jnp.logical_and(group_ref[t] == my_group, shot != t), anch_ref[t], 0)
                limit = jnp.where(lane // ANCH == n, seen, limit)
            scores(8 + c, kbuf[c, 16:20], jnp.where(lane % ANCH < limit, 0.0, DEAD))
        mbuf[...] = jnp.broadcast_to(jnp.max(mbuf[...], axis=1, keepdims=True), (QROWS, HDIM))

        @pl.when(core == 0)
        def _():
            drain(all_v, f_sem)

        lax.fori_loop(0, 4, lambda i, _: (take(vbuf, v_sem, vf_sem, source(i)), 0)[1], 0)

        def product(slot, rows, c, first):
            weights = jnp.exp2(sbuf[slot, rows, :] - mbuf[rows, :1]).astype(jnp.bfloat16)
            vals = vbuf[c, pl.ds(first, 4)].reshape(GROUP, 2 * HDIM)
            return jnp.dot(weights, vals, preferred_element_type=jnp.float32)

        for n in range(4):
            to_x = lax.rem(x + n + 1, 4)
            rows = pl.ds(pl.multiple_of(to_x * QB, QB), QB)
            done = product(8, rows, 0, 16) + product(9, rows, 1, 16)
            for i in range(4):
                done += product(2 * i, rows, core, source(i) * 4)
            if n == 0:
                lax.fori_loop(0, 4, lambda i, _: (drain(halves(vbuf, i, 1 - core), vf_sem.at[i]), 0)[1], 0)
            for i in range(4):
                done += product(2 * i + 1, rows, 1 - core, source(i) * 4)
            blended = done[:, :HDIM] / done[:, HDIM:]
            for k in range(4):
                t = to_x * 4 + k
                slots = ((k * 4 + to_x) * 2 + core) * ROWS + lax.broadcasted_iota(jnp.int32, (ROWS, HDIM), 0)
                piece = jnp.where(slots < live, blended[k * ROWS : (k + 1) * ROWS], 0.0)
                obuf[t] = piece.astype(jnp.bfloat16)
                to_chip(obuf.at[t], out_ref.at[:, columns(head)], os_sem, o_sem, t)

        drain(obuf.at[pl.ds(0, 15)], os_sem)

        drain(kbuf.at[:, pl.ds(0, CHIPS)], asend_sem.at[4])

        drain(anchor_at(kbuf, 0), asend_sem.at[1])
        drain(kbuf.at[0, pl.ds(0, 7)], asend_sem.at[2])
        drain(all_k, asend_sem.at[3])

    @pl.when(seq < 2)
    def _():
        drain(kbuf.at[0, pl.ds(0, HEADS - 1), pl.ds(0, ANCH)], asend_sem.at[0])

    @pl.when(seq == 0)
    def _():
        drain(first_vals, asend_sem.at[5])

    for n in range(9 - AHEAD, 9):
        sent(n // 3, n % 3)
    drain(out_ref, o_sem)


def local(queries, key_rows, values, shot_len, anchor_len, shot_group):
    whole = pl.BlockSpec(memory_space=pl.ANY)
    scalars = pl.BlockSpec(memory_space=pltpu.SMEM)
    dma = pltpu.SemaphoreType.DMA
    flat = (ROWS, HEADS * HDIM)
    out = pl.pallas_call(
        kernel,
        out_shape=jax.ShapeDtypeStruct(flat, jnp.bfloat16),
        in_specs=[scalars] * 3 + [whole] * 3,
        out_specs=whole,
        scratch_shapes=[
            pltpu.VMEM((CHIPS, ROWS, HDIM), jnp.bfloat16),
            pltpu.VMEM((2, 20, ROWS, HDIM), jnp.bfloat16),
            pltpu.VMEM((2, 20, ROWS, 2 * HDIM), jnp.bfloat16),
            pltpu.VMEM((CHIPS, ROWS, HDIM), jnp.bfloat16),
            pltpu.VMEM((10, QROWS, GROUP), jnp.float32),
            pltpu.VMEM((QROWS, HDIM), jnp.float32),
            pltpu.VMEM((ANCH, HEADS * HDIM), jnp.bfloat16),
            dma((3, 3)), dma, dma((4,)), dma((4,)), dma((4,)), dma((4,)),
            dma((4,)), dma((6,)), dma, dma, dma,
        ],
        compiler_params=pltpu.CompilerParams(
            collective_id=0, has_side_effects=True, vmem_limit_bytes=60 * 2**20
        ),
    )(
        shot_len, anchor_len, shot_group,
        queries.reshape(flat), key_rows.reshape(flat), values.reshape(flat),
    )
    return out.reshape(1, *flat)


def solution(mesh):
    spec = P("shot", "seq", None)
    return jax.shard_map(
        local, mesh=mesh, in_specs=(spec, spec, spec, P(), P(), P()), out_specs=spec, check_vma=False
    )
```

```python
import functools
import math

import jax
import jax.numpy as jnp
from jax import lax
from jax.experimental import pallas as pl
from jax.experimental.pallas import tpu as pltpu
from jax.sharding import PartitionSpec as P

MESH = pl.DeviceIdType.MESH
HEADS = 12
HDIM = 128
ANCH = 64
ROWS = 128
CHIPS = 16
SHOTS = 16
GROUP = 512
QROWS = CHIPS * ROWS
QB = 512
QB2 = 256
DEAD = -1e30
AHEAD = 3
SCALE = math.log2(math.e) / math.sqrt(HDIM)


def kernel(
    len_ref, anch_ref, group_ref, q_ref, k_ref, v_ref, out_ref,
    qbuf, kbuf, vbuf, obuf, sbuf, mbuf, first_vals,
    send_sem, q_sem, k_sem, v_sem, kf_sem, vf_sem, a_sem, asend_sem, f_sem, os_sem, o_sem,
):
    shot = lax.axis_index("shot")
    seq = lax.axis_index("seq")
    y, zl = shot // 2, shot % 2
    core, x, zh = seq % 2, (seq // 2) % 4, seq // 8
    here = x * 4 + zh
    is_host = x < 3
    head = zh * 3 + jnp.minimum(x, 2)

    vbuf[:, :, :, HDIM:] = jnp.ones((2, 20, ROWS, HDIM), jnp.bfloat16)

    sibling = (shot, seq + 1 - 2 * core)

    def mate(t):
        return (shot, (lax.rem(t, 4) * 4 + t // 4) * 2 + core)

    def y_peer(k):
        return (lax.rem(y + k, 8) * 2 + zl, seq)

    partner = (y * 2 + 1 - zl, seq)

    barrier = pltpu.get_barrier_semaphore()

    def greet(device):
        pl.semaphore_signal(barrier, inc=1, device_id=device, device_id_type=MESH)

    lax.fori_loop(1, CHIPS, lambda i, _: (greet(mate(lax.rem(here + i, CHIPS))), 0)[1], 0)
    lax.fori_loop(1, 8, lambda i, _: (greet(y_peer(i)), 0)[1], 0)
    greet(sibling)
    greet(partner)
    pl.semaphore_wait(barrier, CHIPS - 1 + 7 + 2)

    def remote(src, dst, ssem, rsem, device):
        return pltpu.make_async_remote_copy(
            src_ref=src, dst_ref=dst, send_sem=ssem, recv_sem=rsem,
            device_id=device, device_id_type=MESH,
        )

    def drain(ref, sem):
        pltpu.make_async_copy(ref, ref, sem).wait()

    def to_chip(src, dst, ssem, rsem, t):
        @pl.when(t == here)
        def _():
            pltpu.make_async_copy(src, dst, rsem).start()

        @pl.when(t != here)
        def _():
            remote(src, dst, ssem, rsem, mate(t)).start()

    def columns(h):
        return pl.ds(pl.multiple_of(h * HDIM, HDIM), HDIM)

    def anchor_at(buf, t):
        return buf.at[(t // 2) % 2, 16 + t // 4, pl.ds(pl.multiple_of((t % 2) * ANCH, ANCH), ANCH), pl.ds(0, HDIM)]

    def pair_at(buf, yy):
        return buf.at[yy % 2, 16 + yy // 2, :, pl.ds(0, HDIM)]

    def anchors_out(src, buf):
        def one(h, _):
            to_chip(src.at[pl.ds(0, ANCH), columns(h)], anchor_at(buf, shot), asend_sem.at[0], a_sem.at[0], lax.rem(h, 3) * 4 + h // 3)
            return 0

        lax.fori_loop(0, HEADS, one, 0)

    @pl.when(seq == 0)
    def _():
        remote(v_ref.at[pl.ds(0, ANCH)], first_vals, asend_sem.at[5], a_sem.at[3], sibling).start()
        anchors_out(k_ref, kbuf)

    def send(kind, turn):
        to_x = lax.rem(x + turn, 3)

        def one(n, _):
            z = lax.rem(zh + 2 + 3 * n, 4)
            h = z * 3 + to_x
            t = to_x * 4 + z
            if kind == 0:
                to_chip(q_ref.at[:, columns(h)], qbuf.at[here], send_sem.at[0, turn], q_sem, t)
            elif kind == 1:
                to_chip(k_ref.at[:, columns(h)], kbuf.at[core, here], send_sem.at[1, turn], k_sem.at[x], t)
            else:
                to_chip(v_ref.at[:, columns(h)], vbuf.at[core, here, :, pl.ds(0, HDIM)], send_sem.at[2, turn], v_sem.at[x], t)
            return 0

        lax.fori_loop(0, 4, one, 0)

    def sent(kind, turn):
        stayed = jnp.logical_and(turn == 0, is_host)

        @pl.when(jnp.logical_not(stayed))
        def _():
            drain(q_ref.at[:, pl.ds(0, 4 * HDIM)], send_sem.at[kind, turn])

        @pl.when(stayed)
        def _():
            drain(q_ref.at[:, pl.ds(0, 3 * HDIM)], send_sem.at[kind, turn])

    def send_next(n):
        sent((n - AHEAD) // 3, (n - AHEAD) % 3)
        send(n // 3, n % 3)

    for n in range(AHEAD):
        send(n // 3, n % 3)

    @pl.when(seq == 1)
    def _():
        drain(first_vals, a_sem.at[3])
        anchors_out(first_vals, vbuf)

    @pl.when(jnp.logical_not(is_host))
    def _():
        for n in range(AHEAD, 9):
            send_next(n)

    @pl.when(is_host)
    def _():
        all_k = kbuf.at[:, pl.ds(16, 4)]
        all_v = vbuf.at[:, pl.ds(16, 4), :, pl.ds(0, HDIM)]

        def anchors_to_partner(buf):
            drain(anchor_at(buf, shot), a_sem.at[0])
            remote(anchor_at(buf, shot), anchor_at(buf, shot), asend_sem.at[1], a_sem.at[1], partner).start()

        def anchors_to_peers(buf):
            drain(anchor_at(buf, y * 2 + 1 - zl), a_sem.at[1])

            def one(i, _):
                remote(pair_at(buf, y), pair_at(buf, y), asend_sem.at[2], a_sem.at[2], y_peer(i)).start()
                return 0

            lax.fori_loop(1, 8, one, 0)

        def anchors_to_sibling(part):
            drain(kbuf.at[0, pl.ds(0, 7)], a_sem.at[2])
            remote(part, part, asend_sem.at[3], f_sem, sibling).start()

        def by_core(step, keys, vals):
            @pl.when(core == 0)
            def _():
                step(keys)

            @pl.when(core == 1)
            def _():
                step(vals)

        by_core(anchors_to_partner, kbuf, vbuf)
        send_next(3)
        by_core(anchors_to_peers, kbuf, vbuf)
        send_next(4)
        send_next(5)

        def source(i):
            return lax.rem(x + 4 - i, 4)

        def halves(buf, g, c):
            return buf.at[c, pl.ds(g * 4, 4), :, pl.ds(0, HDIM)]

        def take(buf, sem, fsem, g):
            drain(halves(buf, g, core), sem.at[g])
            remote(halves(buf, g, core), halves(buf, g, core), asend_sem.at[4], fsem.at[g], sibling).start()

        lane = lax.broadcasted_iota(jnp.int32, (8, GROUP), 1)
        mbuf[...] = jnp.full((QROWS, HDIM), DEAD, jnp.float32)

        def scores(slot, keys, bias):
            keys = keys.reshape(GROUP, HDIM)
            for r in range(0, QROWS, QB):
                rows = qbuf[r // ROWS : (r + QB) // ROWS].reshape(QB, HDIM)
                found = lax.dot_general(rows, keys, (((1,), (1,)), ((), ())), preferred_element_type=jnp.float32)
                found = found * SCALE + bias[:1]
                sbuf[slot, r : r + QB, :] = found
                top = mbuf[r : r + QB, :]
                for c in range(0, GROUP, HDIM):
                    top = jnp.maximum(top, found[:, c : c + HDIM])
                mbuf[r : r + QB, :] = top

        drain(qbuf, q_sem)

        live = len_ref[shot]

        def first(i, _):
            g = source(i)

            @pl.when(i == 0)
            def _():
                send_next(6)

            @pl.when(i == 1)
            def _():
                send_next(7)

            @pl.when(i == 2)
            def _():
                send_next(8)

            take(kbuf, k_sem, kf_sem, g)

            @pl.when(i == 3)
            def _():
                by_core(anchors_to_sibling, all_k, all_v)


            def half(c):
                slot = ((lane // ROWS) * 4 + g) * (2 * ROWS) + c * ROWS + lane % ROWS
                scores(2 * i + jnp.where(c == core, 0, 1), kbuf[c, pl.ds(g * 4, 4)], jnp.where(slot < live, 0.0, DEAD))

            half(core)
            drain(halves(kbuf, g, 1 - core), kf_sem.at[g])
            half(1 - core)
            return 0

        lax.fori_loop(0, 4, first, 0)
        my_group = group_ref[shot]

        @pl.when(core == 1)
        def _():
            drain(all_k, f_sem)

        for c in range(2):
            limit = jnp.zeros((8, GROUP), jnp.int32)
            for n in range(SHOTS // 2):
                t = (n // 2) * 4 + c * 2 + n % 2
                seen = jnp.where(jnp.logical_and(group_ref[t] == my_group, shot != t), anch_ref[t], 0)
                limit = jnp.where(lane // ANCH == n, seen, limit)
            scores(8 + c, kbuf[c, 16:20], jnp.where(lane % ANCH < limit, 0.0, DEAD))
        mbuf[...] = jnp.broadcast_to(jnp.max(mbuf[...], axis=1, keepdims=True), (QROWS, HDIM))

        @pl.when(core == 0)
        def _():
            drain(all_v, f_sem)

        lax.fori_loop(0, 4, lambda i, _: (take(vbuf, v_sem, vf_sem, source(i)), 0)[1], 0)

        def product(slot, rows, c, first):
            weights = jnp.exp2(sbuf[slot, rows, :] - mbuf[rows, :1]).astype(jnp.bfloat16)
            vals = vbuf[c, pl.ds(first, 4)].reshape(GROUP, 2 * HDIM)
            return jnp.dot(weights, vals, preferred_element_type=jnp.float32)

        for n in range(QROWS // QB2):
            to_x = lax.rem(x + n // 2 + 1, 4)
            rows = pl.ds(pl.multiple_of(to_x * QB + n % 2 * QB2, QB2), QB2)
            done = product(8, rows, 0, 16) + product(9, rows, 1, 16)
            for i in range(4):
                done += product(2 * i, rows, core, source(i) * 4)
            if n == 0:
                lax.fori_loop(0, 4, lambda i, _: (drain(halves(vbuf, i, 1 - core), vf_sem.at[i]), 0)[1], 0)
            for i in range(4):
                done += product(2 * i + 1, rows, 1 - core, source(i) * 4)
            blended = done[:, :HDIM] / done[:, HDIM:]
            for k in range(2):
                t = to_x * 4 + n % 2 * 2 + k
                slots = (((n % 2 * 2 + k) * 4 + to_x) * 2 + core) * ROWS + lax.broadcasted_iota(jnp.int32, (ROWS, HDIM), 0)
                piece = jnp.where(slots < live, blended[k * ROWS : (k + 1) * ROWS], 0.0)
                obuf[t] = piece.astype(jnp.bfloat16)
                to_chip(obuf.at[t], out_ref.at[:, columns(head)], os_sem, o_sem, t)

        drain(obuf.at[pl.ds(0, 15)], os_sem)

        drain(kbuf.at[:, pl.ds(0, CHIPS)], asend_sem.at[4])

        drain(anchor_at(kbuf, 0), asend_sem.at[1])
        drain(kbuf.at[0, pl.ds(0, 7)], asend_sem.at[2])
        drain(all_k, asend_sem.at[3])

    @pl.when(seq < 2)
    def _():
        drain(kbuf.at[0, pl.ds(0, HEADS - 1), pl.ds(0, ANCH)], asend_sem.at[0])

    @pl.when(seq == 0)
    def _():
        drain(first_vals, asend_sem.at[5])

    for n in range(9 - AHEAD, 9):
        sent(n // 3, n % 3)
    drain(out_ref, o_sem)


def local(queries, key_rows, values, shot_len, anchor_len, shot_group):
    whole = pl.BlockSpec(memory_space=pl.ANY)
    scalars = pl.BlockSpec(memory_space=pltpu.SMEM)
    dma = pltpu.SemaphoreType.DMA
    flat = (ROWS, HEADS * HDIM)
    out = pl.pallas_call(
        kernel,
        out_shape=jax.ShapeDtypeStruct(flat, jnp.bfloat16),
        in_specs=[scalars] * 3 + [whole] * 3,
        out_specs=whole,
        scratch_shapes=[
            pltpu.VMEM((CHIPS, ROWS, HDIM), jnp.bfloat16),
            pltpu.VMEM((2, 20, ROWS, HDIM), jnp.bfloat16),
            pltpu.VMEM((2, 20, ROWS, 2 * HDIM), jnp.bfloat16),
            pltpu.VMEM((CHIPS, ROWS, HDIM), jnp.bfloat16),
            pltpu.VMEM((10, QROWS, GROUP), jnp.float32),
            pltpu.VMEM((QROWS, HDIM), jnp.float32),
            pltpu.VMEM((ANCH, HEADS * HDIM), jnp.bfloat16),
            dma((3, 3)), dma, dma((4,)), dma((4,)), dma((4,)), dma((4,)),
            dma((4,)), dma((6,)), dma, dma, dma,
        ],
        compiler_params=pltpu.CompilerParams(
            collective_id=0, has_side_effects=True, vmem_limit_bytes=60 * 2**20
        ),
    )(
        shot_len, anchor_len, shot_group,
        queries.reshape(flat), key_rows.reshape(flat), values.reshape(flat),
    )
    return out.reshape(1, *flat)


def solution(mesh):
    spec = P("shot", "seq", None)
    return jax.shard_map(
        local, mesh=mesh, in_specs=(spec, spec, spec, P(), P(), P()), out_specs=spec, check_vma=False
    )
```
